512 devices in a mesh: prow: 32 (over z, x), pcol: 16 (over y, core).
Axes of the slice: x: 4, y: 8, z: 8, core: 2. Of those that a mesh axis runs over, the one named last changes fastest.
Arguments:
- matrix: float32 [2, 8192, 4, 4096], P(None, 'prow', None, 'pcol'), may hold values from -40 to 150, as said below
- block_mask: int32 [64, 64], replicated, may hold values from 0 to 1, as said below
- first_panel: int32 [1], replicated, may hold values from 0 to 31
Outputs:
- factored: float32 [2, 8192, 4, 4096], P(None, 'prow', None, 'pcol')
The draws below stay inside these ranges and needn't reach their ends.
Inputs may be any that keep to these rules, and one draw needn't show every extreme that they name: `block_mask`: symmetric, with ones on the diagonal and on the blocks right beside it. `matrix`: entries off the diagonal lie between -40 and 40, diagonal entries between 60 and 150; the symmetric part of the two diagonal blocks of rows and columns k and k + 1 together is positive definite for every k.
All inputs are finite; a program needn't handle non-finite values.
Results may differ from the reference program's by a relative error of at most 0.0003.
Values sent between devices are 32-bit elements; how exact they have to be, the bound alone decides.
A program may use at most 64 MiB of HBM per device.

```python
import math
import jax
import jax.numpy as jnp
from jax import lax

BLOCK = 256
ROWSLOTS = 2
COLSLOTS = 4
NBLK = 64
ORDER = 16384
N_PROW = 32
N_PCOL = 16


def draw_matrix(key, part):
    noise_key, diag_key, profile_key = jax.random.split(key, 3)
    noise = jax.random.truncated_normal(noise_key, -4.0, 4.0, (ORDER, ORDER), jnp.float32)
    floor_values = jnp.exp(jax.random.uniform(diag_key, (ORDER,), jnp.float32, math.log(60.0), math.log(120.0)))
    profile = jnp.exp(jax.random.uniform(profile_key, (ORDER,), jnp.float32, math.log(0.5), math.log(1.5)))
    positions = jnp.arange(ORDER, dtype=jnp.int32)
    places = positions.astype(jnp.float32)
    block_of = positions // BLOCK
    far_blocks = jnp.abs(block_of[:, None] - block_of[None, :]) >= 2
    noise = noise * jnp.where(far_blocks, jnp.float32(8.0), jnp.float32(1.0))
    reach = jnp.float32(BLOCK) * 0.5
    coupling = 10.0 * profile[:, None] * profile[None, :] * jnp.exp(-jnp.abs(places[:, None] - places[None, :]) / reach)
    on_diagonal = floor_values + 10.0 * profile * profile
    assembled = jnp.where(positions[:, None] == positions[None, :], on_diagonal[:, None], coupling + noise)
    return assembled.reshape(ROWSLOTS, ORDER // ROWSLOTS, COLSLOTS, ORDER // COLSLOTS)


def draw_block_mask(key, part):
    scores = jax.random.randint(key, (NBLK, NBLK), 0, 4 * NBLK)
    rows_index = jnp.arange(NBLK, dtype=jnp.int32)[:, None]
    cols_index = jnp.arange(NBLK, dtype=jnp.int32)[None, :]
    mirrored = jnp.where(rows_index >= cols_index, scores, scores.T)
    filled = (mirrored < 2 * NBLK + rows_index + cols_index) | (jnp.abs(rows_index - cols_index) <= 1)
    return filled.astype(jnp.int32)


def setup_inputs(seed: int = 0) -> dict:
    keys = jax.random.split(jax.random.key(seed), 4)
    return {
        "matrix": draw_matrix(jax.random.fold_in(keys[3], 71), 0),
        "block_mask": draw_block_mask(jax.random.fold_in(keys[3], 71), 0),
        "first_panel": jax.random.randint(keys[2], (1,), 0, NBLK // 2).astype(jnp.int32),
    }


def reference(matrix, block_mask, first_panel):
    blocks = matrix.reshape(NBLK, BLOCK, NBLK, BLOCK)
    block_ids = jnp.arange(NBLK, dtype=jnp.int32)
    kept_blocks = (block_mask == 1) & (block_ids[:, None] >= block_ids[None, :])
    blocks = jnp.where(kept_blocks[:, None, :, None], blocks, jnp.float32(0.0))
    identity = jnp.eye(BLOCK, dtype=jnp.float32)
    for offset in range(2):
        panel_index = first_panel[0] + offset
        column = lax.dynamic_index_in_dim(blocks, panel_index, 2, keepdims=False)
        diagonal_in = lax.dynamic_index_in_dim(column, panel_index, 0, keepdims=False)
        diag_lower = jnp.linalg.cholesky(diagonal_in + identity)
        below_panel = block_ids > panel_index
        raw_panel = jnp.where(below_panel[:, None, None], column, jnp.float32(0.0))
        flattened = raw_panel.reshape(NBLK * BLOCK, BLOCK).T
        solved = jax.scipy.linalg.solve_triangular(diag_lower, flattened, lower=True)
        solved = solved.T.reshape(NBLK, BLOCK, BLOCK)
        renewed = jnp.where(below_panel[:, None, None], solved, jnp.where((block_ids == panel_index)[:, None, None], diag_lower[None], column))
        blocks = lax.dynamic_update_index_in_dim(blocks, renewed, panel_index, 2)
        active = below_panel[:, None] & below_panel[None, :] & (block_ids[:, None] >= block_ids[None, :])
        update = jnp.einsum('iab,jcb->iajc', solved, solved, precision=lax.Precision.HIGHEST)
        blocks = jnp.where(active[:, None, :, None], blocks - update, blocks)
    return blocks.reshape(ROWSLOTS, N_PROW * BLOCK, COLSLOTS, N_PCOL * BLOCK)
```

```python
import functools
import jax
import jax.numpy as jnp
from jax import lax
from jax.experimental import pallas as pl
from jax.experimental.pallas import tpu as pltpu
from jax.sharding import PartitionSpec as P

MESH = pl.DeviceIdType.MESH
HI = lax.Precision.HIGHEST
F32 = jnp.float32
B = 256
NB = 16


def piece_row(c):
    return NB * ((c % 2) * 8 + ((c // 2) % 2) * 4 + c // 4)


def tdot(a, b):
    return lax.dot_general(a, b, (((0,), (0,)), ((), ())), precision=HI, preferred_element_type=F32)


def ndot(a, b):
    return lax.dot_general(a, b, (((1,), (1,)), ((), ())), precision=HI, preferred_element_type=F32)


def inverse_factor(m, w, hook):
    rows = lax.broadcasted_iota(jnp.int32, (NB, 128), 0)
    lane = lax.broadcasted_iota(jnp.int32, (NB, B), 1)
    sub = lax.broadcasted_iota(jnp.int32, (NB, B), 0)
    nxt = m[0:NB, :]
    for p in range(B // NB):
        p0, q = p * NB, p * NB + NB
        inside = (lane >= p0) & (lane < q)
        t = [jnp.broadcast_to(nxt[:, p0 + c : p0 + c + 1], (NB, 128)) for c in range(NB)]
        x = jnp.where(inside, jnp.where(lane - p0 == sub, 1.0, 0.0), nxt)
        x0, x1 = x[:, :128], x[:, 128:]
        s = jnp.ones((NB, 128), F32)
        for j in range(NB):
            d = jnp.broadcast_to(t[j][j : j + 1, :], (NB, 128))
            s = jnp.where(rows == j, lax.rsqrt(d), s)
            mm = jnp.where(rows > j, t[j], 0.0) * (1.0 / d)
            for c in range(j + 1, NB):
                t[c] = t[c] - mm * jnp.broadcast_to(t[c][j : j + 1, :], (NB, 128))
            x0 = x0 - mm * jnp.broadcast_to(x0[j : j + 1, :], (NB, 128))
            x1 = x1 - mm * jnp.broadcast_to(x1[j : j + 1, :], (NB, 128))
        rr = jnp.concatenate([x0 * s, x1 * s], axis=1)
        w[p0:q, :] = jnp.where(lane < q, rr, 0.0)
        if q < B:
            nxt = jnp.where(inside, 0.0, m[q : q + NB, :]) - tdot(rr[:, q : q + NB], rr)
        if q + NB < B:
            wide = lax.broadcasted_iota(jnp.int32, (B - q - NB, B), 1)
            rest = m[q + NB :, :]
            m[q + NB :, :] = jnp.where((wide >= p0) & (wide < q), 0.0, rest) - tdot(rr[:, q + NB :], rr)
        hook(p)


def gather_kernel(
    k_ref, x_ref, e_ref, rows_ref, cols_ref, fac_ref,
    rsb, hb, own, low, g12, work,
    rs_s, rs_r, g_s, g_r, cs_s, cs_r, ag_s, ag_r, sib_s, sib_r, zc_s, zc_r, xc_s, xc_r, xf_s, xf_r,
    w_s, w_r, loc,
):
    r, c = lax.axis_index("prow"), lax.axis_index("pcol")
    z, x, y, h = r // 4, r % 4, c // 2, c % 2
    k = k_ref[0]
    cand = (r % 16) == c
    u, rest = r // 16, r % 16
    to_col = (c + 16 * u, rest)
    below = (r + 31) % 32
    home = (below, below % 16)
    is_sub = ((r + 31) % 16) == c

    def at(dz=0, dx=0, dy=0, core=None):
        zz, xx, yy = (z + dz) % 8, (x + dx) % 4, (y + dy) % 8
        return (zz * 4 + xx, yy * 2 + (h if core is None else core))

    def relay_y(zz, m):
        return (2 * zz + m // 2 + 3 + zz // 4) % 8

    is_holder = (x < 3) & (y == relay_y(z, x))

    def remote(src, dst, ss, rs, to):
        return pltpu.make_async_remote_copy(
            src_ref=src, dst_ref=dst, send_sem=ss, recv_sem=rs, device_id=to, device_id_type=MESH
        )

    def drain(ref, sem):
        pltpu.make_async_copy(ref, ref, sem).wait()

    bar = pltpu.get_barrier_semaphore()

    def greet(to):
        pl.semaphore_signal(bar, inc=1, device_id=to, device_id_type=MESH)

    for j in range(1, 16):
        greet((r, (c + j) % 16))
    for j in range(1, 8):
        greet(at(dz=j))
    for j in range(1, 4):
        greet(at(dx=j))

    @pl.when(jnp.logical_not(cand))
    def _():
        greet((c + 16 * u, rest))

    @pl.when(cand)
    def _():
        up = (r + 1) % 32
        greet((up, up % 16))
        greet((up, r % 16))

    @pl.when(is_holder)
    def _():
        def one(i, carry):
            greet((i, i % 16))
            return carry

        lax.fori_loop(0, 32, one, 0)

    arrivals = 15 + 7 + 3 + jnp.where(cand, 49, 1) + jnp.where(is_sub, 1, 0)
    mine = pl.ds(pl.multiple_of(piece_row(c), NB), NB)

    def first_sends():
        pl.semaphore_wait(bar, arrivals)

        @pl.when(is_sub)
        def _():
            remote(e_ref.at[1], g12.at[0], g_s.at[0], g_r.at[0], home).start()

        @pl.when(cand)
        def _():
            remote(e_ref.at[2], g12.at[1], g_s.at[1], g_r.at[1], home).start()

        for j in range(1, 16):
            to = (c + j) % 16
            row = pl.multiple_of(piece_row(to), NB)
            remote(x_ref.at[:, pl.ds(row, NB), :], rsb.at[c], rs_s, rs_r, (r, to)).start()

    rsb[c] = x_ref[:, mine, :]
    theirs = pl.ds(pl.multiple_of(piece_row(rest), NB), NB)

    def pick_rows():
        drain(rsb.at[pl.ds(0, 15)], rs_r)
        rows_ref[0, :, mine, :] = rsb[k % 16]
        rows_ref[1, :, mine, :] = rsb[(k + 1) % 16]
        piece = rows_ref.at[:, :, mine, :]

        @pl.when(jnp.logical_not(cand))
        def _():
            remote(piece, cols_ref.at[u, :, :, mine, :], cs_s, cs_r, to_col).start()

        @pl.when(cand)
        def _():
            cols_ref[u, :, :, mine, :] = rows_ref[:, :, mine, :]

        for j in range(1, 8):
            remote(piece, piece, ag_s, ag_r, at(dy=j)).start()

    def send_z():
        piece = cols_ref.at[u, :, :, theirs, :]

        @pl.when(jnp.logical_not(cand))
        def _():
            drain(piece, cs_r)

        for j in range(1, 8):
            remote(piece, piece, zc_s, zc_r, at(dz=j)).start()

    def send_sibling():
        drain(rows_ref.at[:, :, pl.ds(0, 7 * NB), :], ag_r)
        half = rows_ref.at[:, :, pl.ds(pl.multiple_of(128 * h, 128), 128), :]
        remote(half, half, sib_s, sib_r, at(core=1 - h)).start()

    def quarter(xx):
        return pl.ds(pl.multiple_of(NB * (8 * (xx % 2) + 4 * ((xx // 2) % 2)), 64), 64)

    def send_x():
        drain(cols_ref.at[0, :, :, pl.ds(0, 7 * NB), :], zc_r)
        part = cols_ref.at[:, :, :, quarter(x), :]
        remote(part, part, xc_s.at[0], xc_r.at[0], at(dx=1)).start()
        remote(part, part, xc_s.at[1], xc_r.at[1], at(dx=3)).start()

    def forward_x():
        for way, dx in ((0, 1), (1, 3)):
            part = cols_ref.at[:, :, :, quarter(x + 4 - dx), :]
            drain(part, xc_r.at[way])
            half = cols_ref.at[way, :, :, quarter(x + 4 - dx), :]
            remote(half, half, xf_s.at[way], xf_r.at[way], at(dx=dx)).start()

    def scatter_factor(m, pieces=range(16)):
        for p in pieces:
            zz, core = p % 8, p // 8
            to = (zz * 4 + m, relay_y(zz, m) * 2 + core)
            remote(low.at[m, pl.ds(p * NB, NB), :], hb.at[r], w_s.at[m, 0], w_r.at[m, 0], to).start()

    slab = pl.ds(pl.multiple_of(128 * h + NB * z, NB), NB)

    def relay_factor(m, stage):
        piece = fac_ref.at[m, slab, :]
        if stage == 0:

            @pl.when(is_holder & (x == m))
            def _():
                drain(hb, w_r.at[m, 0])
                fac_ref[m, slab, :] = hb[k]
                for j in range(1, 4):
                    remote(piece, piece, w_s.at[m, 1], w_r.at[m, 1], at(dx=j)).start()

        elif stage == 1:

            @pl.when(y == relay_y(z, m))
            def _():
                @pl.when(x != m)
                def _():
                    drain(piece, w_r.at[m, 1])

                for j in range(1, 8):
                    remote(piece, piece, w_s.at[m, 2], w_r.at[m, 2], at(dy=j)).start()

        elif stage == 2:

            @pl.when(y != relay_y(z, m))
            def _():
                drain(piece, w_r.at[m, 2])

            for j in range(1, 8):
                remote(piece, piece, w_s.at[m, 3], w_r.at[m, 3], at(dz=j)).start()
        elif stage == 3:
            drain(fac_ref.at[m, pl.ds(0, 7 * NB), :], w_r.at[m, 3])
            half = fac_ref.at[m, pl.ds(pl.multiple_of(128 * h, 128), 128), :]
            remote(half, half, w_s.at[m, 4], w_r.at[m, 4], at(core=1 - h)).start()

    eye = jnp.where(
        lax.broadcasted_iota(jnp.int32, (B, B), 0) == lax.broadcasted_iota(jnp.int32, (B, B), 1), 1.0, 0.0
    ).astype(F32)

    @pl.when(cand)
    def _():
        a = e_ref[0]
        work[...] = (a + a.T) * 0.5 + eye

        def first_hook(p):
            if p == 4:
                first_sends()
                scatter_factor(0, range(5))
            elif p > 4:
                scatter_factor(0, [p])

        inverse_factor(work, low.at[0], first_hook)
        drain(g12.at[0], g_r.at[0])
        drain(g12.at[1], g_r.at[1])
        l21 = ndot(g12[0], low[0])
        low[1] = l21
        scatter_factor(1)
        d = g12[1]
        work[...] = (d + d.T) * 0.5 + eye - ndot(l21, l21)

        def second_hook(p):
            scatter_factor(2, [p])
            if p == 2:
                pick_rows()
            if p == 7:
                send_z()
            if p == 10:
                relay_factor(0, 1)
            if p == 12:
                relay_factor(1, 1)
            if p == 15:
                relay_factor(0, 2)

        inverse_factor(work, low.at[2], second_hook)
        relay_factor(1, 2)
        send_sibling()

    @pl.when(jnp.logical_not(cand))
    def _():
        first_sends()
        pick_rows()
        send_z()
        for stage in range(3):
            for m in range(2):
                relay_factor(m, stage)
        send_sibling()

    relay_factor(0, 3)
    relay_factor(1, 3)
    relay_factor(2, 0)
    send_x()
    relay_factor(2, 1)
    relay_factor(2, 2)
    relay_factor(2, 3)
    forward_x()

    for m in range(3):
        drain(fac_ref.at[m, pl.ds(0, 128), :], w_r.at[m, 4])
    drain(rows_ref.at[:, :, pl.ds(0, 128), :], sib_r)
    for way, dx in ((0, 1), (1, 3)):
        drain(cols_ref.at[way, :, :, quarter(x + 2), :], xf_r.at[way])

    @pl.when(is_sub)
    def _():
        drain(e_ref.at[1], g_s.at[0])

    @pl.when(cand)
    def _():
        drain(e_ref.at[2], g_s.at[1])
        for m in range(3):
            drain(low.at[m], w_s.at[m, 0])

    drain(rsb.at[pl.ds(0, 15)], rs_s)

    @pl.when(jnp.logical_not(cand))
    def _():
        drain(rows_ref.at[:, :, mine, :], cs_s)

    drain(rows_ref.at[:, :, pl.ds(0, 7 * NB), :], ag_s)
    drain(rows_ref.at[:, :, pl.ds(0, 128), :], sib_s)
    drain(cols_ref.at[0, :, :, pl.ds(0, 7 * NB), :], zc_s)
    for way in range(2):
        drain(cols_ref.at[:, :, :, quarter(x), :], xc_s.at[way])
        drain(cols_ref.at[way, :, :, quarter(x), :], xf_s.at[way])
    for m in range(3):

        @pl.when(is_holder & (x == m))
        def _():
            drain(fac_ref.at[m, pl.ds(0, 3 * NB), :], w_s.at[m, 1])

        @pl.when(y == relay_y(z, m))
        def _():
            drain(fac_ref.at[m, pl.ds(0, 7 * NB), :], w_s.at[m, 2])

        drain(fac_ref.at[m, pl.ds(0, 7 * NB), :], w_s.at[m, 3])
        drain(fac_ref.at[m, pl.ds(0, 128), :], w_s.at[m, 4])


def split(a):
    hi = a.astype(jnp.bfloat16)
    return hi, (a - hi.astype(F32)).astype(jnp.bfloat16)


def dot3(a, b):
    dims = (((1,), (1,)), ((), ()))
    one = lambda u, v: lax.dot_general(u, v, dims, preferred_element_type=F32)
    return one(a[0], b[0]) + (one(a[0], b[1]) + one(a[1], b[0]))


def update_kernel(k_ref, mask_ref, m_ref, rows_ref, cols_ref, fac_ref, out_ref, l1h, l1l, l2h, l2l):
    r, c = lax.axis_index("prow"), lax.axis_index("pcol")
    k = k_ref[0]
    n = k + 1
    w1, l21, w2 = split(fac_ref[0]), split(fac_ref[1]), split(fac_ref[2])

    ids = [r, r + 32, c, c + 32, c + 16, c + 48]
    for v, i in enumerate(ids):
        if v < 2:
            a1, a2 = rows_ref[0, v], rows_ref[1, v]
        else:
            a1, a2 = cols_ref[v // 2 - 1, 0, v % 2], cols_ref[v // 2 - 1, 1, v % 2]
        a1 = jnp.where((mask_ref[i, k] == 1) & (i > k), a1, 0.0)
        a2 = jnp.where((mask_ref[i, n] == 1) & (i > n), a2, 0.0)
        p1 = split(dot3(split(a1), w1))
        a2 = jnp.where(i > n, a2 - dot3(p1, l21), 0.0)
        p2 = split(dot3(split(a2), w2))
        l1h[v], l1l[v] = p1
        l2h[v], l2l[v] = p2

    col_slot = [2, 4, 3, 5]
    for s in range(2):
        i = r + 32 * s
        for t in range(4):
            j = c + 16 * t
            v = col_slot[t]
            lower = i >= j
            if s == 0 and t >= 2:
                out_ref[s, :, t, :] = jnp.zeros((B, B), F32)
                continue
            base = jnp.where((mask_ref[i, j] == 1) & lower, m_ref[s, :, t, :], 0.0)
            upd = dot3((l1h[s], l1l[s]), (l1h[v], l1l[v])) + dot3((l2h[s], l2l[s]), (l2h[v], l2l[v]))
            out_ref[s, :, t, :] = base - jnp.where(lower, upd, 0.0)

    eye = jnp.where(
        lax.broadcasted_iota(jnp.int32, (B, B), 0) == lax.broadcasted_iota(jnp.int32, (B, B), 1), 1.0, 0.0
    ).astype(F32)
    for s in range(2):
        i = r + 32 * s
        for t in range(3):
            j = c + 16 * t

            @pl.when((j == k) & (i > k))
            def _():
                out_ref[s, :, t, :] = l1h[s].astype(F32) + l1l[s].astype(F32)

            @pl.when((j == n) & (i > n))
            def _():
                out_ref[s, :, t, :] = l2h[s].astype(F32) + l2l[s].astype(F32)

            @pl.when((j == k) & (i == k))
            def _():
                a = m_ref[s, :, t, :]
                f = ndot((a + a.T) * 0.5 + eye, fac_ref[0])
                low = lax.broadcasted_iota(jnp.int32, (B, B), 0) >= lax.broadcasted_iota(jnp.int32, (B, B), 1)
                out_ref[s, :, t, :] = jnp.where(low, f, 0.0)

            @pl.when((j == n) & (i == n))
            def _():
                a = m_ref[s, :, t, :]
                g = fac_ref[1]
                f = ndot((a + a.T) * 0.5 + eye - ndot(g, g), fac_ref[2])
                low = lax.broadcasted_iota(jnp.int32, (B, B), 0) >= lax.broadcasted_iota(jnp.int32, (B, B), 1)
                out_ref[s, :, t, :] = jnp.where(low, f, 0.0)


def vmem():
    return pl.BlockSpec(memory_space=pltpu.VMEM)


def smem():
    return pl.BlockSpec(memory_space=pltpu.SMEM)


def local(matrix, block_mask, first_panel):
    r, c = lax.axis_index("prow"), lax.axis_index("pcol")
    k = first_panel[0]
    t = jnp.where(c == k % 16, k // 16, (k + 1) // 16)
    x = lax.dynamic_index_in_dim(matrix, t, 2, keepdims=False)

    def block(s, t):
        return lax.dynamic_slice(matrix, (s, 0, t, 0), (1, B, 1, B)).reshape(B, B)

    top = (r == 0).astype(jnp.int32)
    e = jnp.stack([block(0, r // 16), block(top, (r - 1 + 32 * top) // 16), block(top, r // 16 + 2 * top)])
    dma = pltpu.SemaphoreType.DMA
    rows, cols, fac = pl.pallas_call(
        gather_kernel,
        out_shape=(
            jax.ShapeDtypeStruct((2, 2, B, B), F32),
            jax.ShapeDtypeStruct((2, 2, 2, B, B), F32),
            jax.ShapeDtypeStruct((3, B, B), F32),
        ),
        in_specs=[smem(), vmem(), vmem()],
        out_specs=(vmem(), vmem(), vmem()),
        scratch_shapes=[
            pltpu.VMEM((16, 2, NB, B), F32),
            pltpu.VMEM((32, NB, B), F32),
            pltpu.VMEM((8, 128), F32),
            pltpu.VMEM((3, B, B), F32),
            pltpu.VMEM((2, B, B), F32),
            pltpu.VMEM((B, B), F32),
            dma, dma, dma((2,)), dma((2,)), dma, dma, dma, dma, dma, dma, dma, dma,
            dma((2,)), dma((2,)), dma((2,)), dma((2,)), dma((3, 5)), dma((3, 5)), dma,
        ],
        compiler_params=pltpu.CompilerParams(collective_id=0, has_side_effects=True, vmem_limit_bytes=40 << 20),
        cost_estimate=pl.CostEstimate(flops=10**9, bytes_accessed=10**7, transcendentals=0),
        name="gather_factor",
    )(first_panel, x, e)
    return pl.pallas_call(
        update_kernel,
        out_shape=jax.ShapeDtypeStruct(matrix.shape, F32),
        in_specs=[smem(), smem(), vmem(), vmem(), vmem(), vmem()],
        out_specs=vmem(),
        scratch_shapes=[pltpu.VMEM((6, B, B), jnp.bfloat16)] * 4,
        compiler_params=pltpu.CompilerParams(vmem_limit_bytes=48 << 20),
        cost_estimate=pl.CostEstimate(flops=4 * 10**9, bytes_accessed=10**7, transcendentals=0),
        name="update",
    )(first_panel, block_mask, matrix, rows, cols, fac)


def solution(mesh):
    spec = P(None, "prow", None, "pcol")
    return jax.shard_map(local, mesh=mesh, in_specs=(spec, P(), P()), out_specs=spec, check_vma=False)
```

```python
import functools
import jax
import jax.numpy as jnp
from jax import lax
from jax.experimental import pallas as pl
from jax.experimental.pallas import tpu as pltpu
from jax.sharding import PartitionSpec as P

MESH = pl.DeviceIdType.MESH
HI = lax.Precision.HIGHEST
F32 = jnp.float32
B = 256
NB = 16


def piece_row(c):
    return NB * ((c % 2) * 8 + ((c // 2) % 2) * 4 + c // 4)


def tdot(a, b):
    return lax.dot_general(a, b, (((0,), (0,)), ((), ())), precision=HI, preferred_element_type=F32)


def ndot(a, b):
    return lax.dot_general(a, b, (((1,), (1,)), ((), ())), precision=HI, preferred_element_type=F32)


def inverse_factor(m, w, hook):
    rows = lax.broadcasted_iota(jnp.int32, (NB, 128), 0)
    lane = lax.broadcasted_iota(jnp.int32, (NB, B), 1)
    sub = lax.broadcasted_iota(jnp.int32, (NB, B), 0)
    nxt = m[0:NB, :]
    for p in range(B // NB):
        p0, q = p * NB, p * NB + NB
        inside = (lane >= p0) & (lane < q)
        t = [jnp.broadcast_to(nxt[:, p0 + c : p0 + c + 1], (NB, 128)) for c in range(NB)]
        x = jnp.where(inside, jnp.where(lane - p0 == sub, 1.0, 0.0), nxt)
        x0, x1 = x[:, :128], x[:, 128:]
        s = jnp.ones((NB, 128), F32)
        for j in range(NB):
            d = jnp.broadcast_to(t[j][j : j + 1, :], (NB, 128))
            s = jnp.where(rows == j, lax.rsqrt(d), s)
            mm = jnp.where(rows > j, t[j], 0.0) * (1.0 / d)
            for c in range(j + 1, NB):
                t[c] = t[c] - mm * jnp.broadcast_to(t[c][j : j + 1, :], (NB, 128))
            x0 = x0 - mm * jnp.broadcast_to(x0[j : j + 1, :], (NB, 128))
            x1 = x1 - mm * jnp.broadcast_to(x1[j : j + 1, :], (NB, 128))
        rr = jnp.concatenate([x0 * s, x1 * s], axis=1)
        w[p0:q, :] = jnp.where(lane < q, rr, 0.0)
        if q < B:
            nxt = jnp.where(inside, 0.0, m[q : q + NB, :]) - tdot(rr[:, q : q + NB], rr)
        if q + NB < B:
            wide = lax.broadcasted_iota(jnp.int32, (B - q - NB, B), 1)
            rest = m[q + NB :, :]
            m[q + NB :, :] = jnp.where((wide >= p0) & (wide < q), 0.0, rest) - tdot(rr[:, q + NB :], rr)
        hook(p)


def gather_kernel(
    k_in, m_ref, rows_ref, cols_ref, fac_ref, blk,
    k_ref, k_sem, xs, rsb0, rsb1, hb, low, g12, work, ld,
    rs_s, rs_r, g_s, g_r, cs_s, cs_r, ag_s, ag_r, sib_s, sib_r, zc_s, zc_r, xc_s, xc_r, xf_s, xf_r,
    w_s, w_r,
):
    rsb = (rsb0, rsb1)
    r, c = lax.axis_index("prow"), lax.axis_index("pcol")
    z, x, y, h = r // 4, r % 4, c // 2, c % 2
    cand = (r % 16) == c
    u, rest = r // 16, r % 16
    to_col = (c + 16 * u, rest)
    below = (r + 31) % 32
    home = (below, below % 16)
    is_sub = ((r + 31) % 16) == c

    def at(dz=0, dx=0, dy=0, core=None):
        zz, xx, yy = (z + dz) % 8, (x + dx) % 4, (y + dy) % 8
        return (zz * 4 + xx, yy * 2 + (h if core is None else core))

    def relay_y(zz, m):
        return (2 * zz + (5, 3)[m] + zz // 4) % 8

    on_line = (y == relay_y(z, 0), y == relay_y(z, 1))
    first_holder = on_line[0] & (x == 0)

    def remote(src, dst, ss, rs, to):
        return pltpu.make_async_remote_copy(
            src_ref=src, dst_ref=dst, send_sem=ss, recv_sem=rs, device_id=to, device_id_type=MESH
        )

    def drain(ref, sem):
        pltpu.make_async_copy(ref, ref, sem).wait()

    k_copy = pltpu.make_async_copy(k_in, k_ref, k_sem)
    k_copy.start()
    loads = [
        pltpu.make_async_copy(m_ref.at[s, :, t, :], blk.at[s, t], ld.at[s, t])
        for t in range(4) for s in range(2)
    ]
    for cp in loads:
        cp.start()
    top = jnp.where(r == 0, 1, 0)
    sub_block = blk.at[top, (below) // 16]
    next_block = blk.at[top, r // 16 + 2 * top]
    bar = pltpu.get_barrier_semaphore()

    def greet(to):
        pl.semaphore_signal(bar, inc=1, device_id=to, device_id_type=MESH)

    for j in range(1, 16):
        greet((r, (c + j) % 16))
    for j in range(1, 8):
        greet(at(dz=j))
    for j in range(1, 4):
        greet(at(dx=j))

    @pl.when(jnp.logical_not(cand))
    def _():
        greet((c + 16 * u, rest))

    @pl.when(cand)
    def _():
        up = (r + 1) % 32
        greet((up, up % 16))
        greet((up, r % 16))

    @pl.when(first_holder | on_line[1])
    def _():
        def one(i, carry):
            greet((i, i % 16))
            return carry

        lax.fori_loop(0, 32, one, 0)

    arrivals = 15 + 7 + 3 + jnp.where(cand, 81, 1) + jnp.where(is_sub, 1, 0)
    mine = pl.ds(pl.multiple_of(piece_row(c), NB), NB)

    def first_sends():
        pl.semaphore_wait(bar, arrivals)

        @pl.when(is_sub)
        def _():
            remote(sub_block, g12.at[0], g_s.at[0], g_r.at[0], home).start()

        @pl.when(cand)
        def _():
            remote(next_block, g12.at[1], g_s.at[1], g_r.at[1], home).start()

        for s in range(2):
            for j in range(1, 16):
                to = (c + j) % 16
                row = pl.multiple_of(piece_row(to), NB)
                remote(xs.at[s, pl.ds(row, NB), :], rsb[s].at[c], rs_s.at[s], rs_r.at[s], (r, to)).start()

    for cp in loads:
        cp.wait()
    k_copy.wait()
    k = k_ref[0]
    slot = jnp.where(c == k % 16, k // 16, (k + 1) // 16)
    xs[...] = blk[:, slot]
    rsb0[c] = xs[0, mine, :]
    rsb1[c] = xs[1, mine, :]
    theirs = pl.ds(pl.multiple_of(piece_row(rest), NB), NB)

    def pick_rows(s):
        drain(rsb[s].at[pl.ds(0, 15)], rs_r.at[s])
        rows_ref[0, s, mine, :] = rsb[s][k % 16]
        rows_ref[1, s, mine, :] = rsb[s][(k + 1) % 16]

        @pl.when(jnp.logical_not(cand))
        def _():
            piece = rows_ref.at[:, s, mine, :]
            remote(piece, cols_ref.at[u, :, s, mine, :], cs_s.at[s], cs_r.at[s], to_col).start()

        @pl.when(cand)
        def _():
            cols_ref[u, :, s, mine, :] = rows_ref[:, s, mine, :]

    def send_y():
        piece = rows_ref.at[:, :, mine, :]
        for j in range(1, 8):
            remote(piece, piece, ag_s, ag_r, at(dy=j)).start()

    def send_z(s):
        piece = cols_ref.at[u, :, s, theirs, :]

        @pl.when(jnp.logical_not(cand))
        def _():
            drain(piece, cs_r.at[s])

        for j in range(1, 8):
            remote(piece, piece, zc_s.at[s], zc_r.at[s], at(dz=j)).start()

    def send_sibling():
        drain(rows_ref.at[:, :, pl.ds(0, 7 * NB), :], ag_r)
        half = rows_ref.at[:, :, pl.ds(pl.multiple_of(128 * h, 128), 128), :]
        remote(half, half, sib_s, sib_r, at(core=1 - h)).start()

    def quarter(xx):
        return pl.ds(pl.multiple_of(NB * (8 * (xx % 2) + 4 * ((xx // 2) % 2)), 64), 64)

    def send_x(s):
        drain(cols_ref.at[0, :, s, pl.ds(0, 7 * NB), :], zc_r.at[s])
        part = cols_ref.at[:, :, s, quarter(x), :]
        remote(part, part, xc_s.at[s, 0], xc_r.at[s, 0], at(dx=1)).start()
        remote(part, part, xc_s.at[s, 1], xc_r.at[s, 1], at(dx=3)).start()

    def forward_x(s):
        for way, dx in ((0, 1), (1, 3)):
            part = cols_ref.at[:, :, s, quarter(x + 4 - dx), :]
            drain(part, xc_r.at[s, way])
            half = cols_ref.at[way, :, s, quarter(x + 4 - dx), :]
            remote(half, half, xf_s.at[s, way], xf_r.at[s, way], at(dx=dx)).start()

    def scatter_factor(f, pieces=range(16)):
        for p in pieces:
            zz, core = p % 8, p // 8
            src = low.at[f, pl.ds(p * NB, NB), :]
            if f < 2:
                to = (zz * 4, relay_y(zz, 0) * 2 + core)
                remote(src, hb.at[f, r], w_s.at[0, f], w_r.at[0, f], to).start()
            else:
                for xx in range(4):
                    to = (zz * 4 + xx, relay_y(zz, 1) * 2 + core)
                    remote(src, hb.at[0, r], w_s.at[1, 0], w_r.at[1, 0], to).start()

    slab = pl.ds(pl.multiple_of(128 * h + NB * z, NB), NB)
    side = pl.ds(pl.multiple_of(128 * h, 128), 128)

    def relay_first(stage):
        piece = fac_ref.at[pl.ds(0, 2), slab, :]
        if stage == 0:

            @pl.when(first_holder)
            def _():
                drain(hb.at[0], w_r.at[0, 0])
                drain(hb.at[1], w_r.at[0, 1])
                fac_ref[0, slab, :] = hb[0, k]
                fac_ref[1, slab, :] = hb[1, k]
                for j in range(1, 4):
                    remote(piece, piece, w_s.at[0, 2], w_r.at[0, 2], at(dx=j)).start()

        elif stage == 1:

            @pl.when(on_line[0])
            def _():
                @pl.when(x != 0)
                def _():
                    drain(piece, w_r.at[0, 2])

                for j in range(1, 8):
                    remote(piece, piece, w_s.at[0, 3], w_r.at[0, 3], at(dy=j)).start()

        elif stage == 2:

            @pl.when(jnp.logical_not(on_line[0]))
            def _():
                drain(piece, w_r.at[0, 3])

            for j in range(1, 8):
                remote(piece, piece, w_s.at[0, 4], w_r.at[0, 4], at(dz=j)).start()
        else:
            drain(fac_ref.at[pl.ds(0, 2), pl.ds(0, 7 * NB), :], w_r.at[0, 4])
            half = fac_ref.at[pl.ds(0, 2), side, :]
            remote(half, half, w_s.at[0, 5], w_r.at[0, 5], at(core=1 - h)).start()

    def relay_last(stage):
        piece = fac_ref.at[2, slab, :]
        if stage == 0:

            @pl.when(on_line[1])
            def _():
                drain(hb.at[0], w_r.at[1, 0])
                fac_ref[2, slab, :] = hb[0, k]
                for j in range(1, 8):
                    remote(piece, piece, w_s.at[1, 3], w_r.at[1, 3], at(dy=j)).start()

        elif stage == 1:

            @pl.when(jnp.logical_not(on_line[1]))
            def _():
                drain(piece, w_r.at[1, 3])

            for j in range(1, 8):
                remote(piece, piece, w_s.at[1, 4], w_r.at[1, 4], at(dz=j)).start()
        else:
            drain(fac_ref.at[2, pl.ds(0, 7 * NB), :], w_r.at[1, 4])
            half = fac_ref.at[2, side, :]
            remote(half, half, w_s.at[1, 5], w_r.at[1, 5], at(core=1 - h)).start()

    eye = jnp.where(
        lax.broadcasted_iota(jnp.int32, (B, B), 0) == lax.broadcasted_iota(jnp.int32, (B, B), 1), 1.0, 0.0
    ).astype(F32)

    @pl.when(cand)
    def _():
        a = blk[0, r // 16]
        work[...] = (a + a.T) * 0.5 + eye

        def first_hook(p):
            if p == 4:
                first_sends()
                scatter_factor(0, range(5))
            elif p > 4:
                scatter_factor(0, [p])

        inverse_factor(work, low.at[0], first_hook)
        drain(g12.at[0], g_r.at[0])
        drain(g12.at[1], g_r.at[1])
        l21 = ndot(g12[0], low[0])
        low[1] = l21
        scatter_factor(1)
        d = g12[1]
        work[...] = (d + d.T) * 0.5 + eye - ndot(l21, l21)

        pick_rows(0)

        def second_hook(p):
            scatter_factor(2, [p])
            for when, step in plan:
                if when == p:
                    step()

        plan = (
            (1, lambda: pick_rows(1)),
            (2, send_y),
            (3, lambda: send_z(0)),
            (7, lambda: send_z(1)),
            (10, lambda: relay_first(1)),
            (12, lambda: send_x(0)),
            (15, lambda: relay_first(2)),
        )
        inverse_factor(work, low.at[2], second_hook)

    @pl.when(jnp.logical_not(cand))
    def _():
        first_sends()
        pick_rows(0)
        pick_rows(1)
        send_y()
        send_z(0)
        send_z(1)
        relay_first(0)
        relay_first(1)
        send_x(0)
        relay_first(2)

    send_x(1)
    send_sibling()
    forward_x(0)
    relay_first(3)
    relay_last(0)
    relay_last(1)
    forward_x(1)
    relay_last(2)

    drain(fac_ref.at[pl.ds(0, 2), pl.ds(0, 128), :], w_r.at[0, 5])
    drain(fac_ref.at[2, pl.ds(0, 128), :], w_r.at[1, 5])
    drain(rows_ref.at[:, :, pl.ds(0, 128), :], sib_r)
    for s in range(2):
        for way in range(2):
            drain(cols_ref.at[way, :, s, quarter(x + 2), :], xf_r.at[s, way])

    @pl.when(is_sub)
    def _():
        drain(g12.at[0], g_s.at[0])

    @pl.when(cand)
    def _():
        drain(g12.at[0], g_s.at[1])
        drain(low.at[0], w_s.at[0, 0])
        drain(low.at[0], w_s.at[0, 1])
        drain(hb.at[:, pl.ds(0, 32)], w_s.at[1, 0])

    drain(rows_ref.at[:, :, pl.ds(0, 7 * NB), :], ag_s)
    drain(rows_ref.at[:, :, pl.ds(0, 128), :], sib_s)
    for s in range(2):
        drain(rsb[s].at[pl.ds(0, 15)], rs_s.at[s])

        @pl.when(jnp.logical_not(cand))
        def _():
            drain(rows_ref.at[:, s, mine, :], cs_s.at[s])

        drain(cols_ref.at[0, :, s, pl.ds(0, 7 * NB), :], zc_s.at[s])
        for way in range(2):
            drain(cols_ref.at[:, :, s, quarter(x), :], xc_s.at[s, way])
            drain(cols_ref.at[way, :, s, quarter(x), :], xf_s.at[s, way])

    @pl.when(first_holder)
    def _():
        drain(fac_ref.at[pl.ds(0, 2), pl.ds(0, 3 * NB), :], w_s.at[0, 2])

    @pl.when(on_line[0])
    def _():
        drain(fac_ref.at[pl.ds(0, 2), pl.ds(0, 7 * NB), :], w_s.at[0, 3])

    @pl.when(on_line[1])
    def _():
        drain(fac_ref.at[2, pl.ds(0, 7 * NB), :], w_s.at[1, 3])

    drain(fac_ref.at[pl.ds(0, 2), pl.ds(0, 7 * NB), :], w_s.at[0, 4])
    drain(fac_ref.at[2, pl.ds(0, 7 * NB), :], w_s.at[1, 4])
    drain(fac_ref.at[pl.ds(0, 2), pl.ds(0, 128), :], w_s.at[0, 5])
    drain(fac_ref.at[2, pl.ds(0, 128), :], w_s.at[1, 5])


def split(a):
    hi = a.astype(jnp.bfloat16)
    return hi, (a - hi.astype(F32)).astype(jnp.bfloat16)


def dot3(a, b):
    dims = (((1,), (1,)), ((), ()))
    one = lambda u, v: lax.dot_general(u, v, dims, preferred_element_type=F32)
    return one(a[0], b[0]) + (one(a[0], b[1]) + one(a[1], b[0]))


def update_kernel(k_ref, mask_ref, m_ref, rows_ref, cols_ref, fac_ref, out_ref, l1h, l1l, l2h, l2l):
    r, c = lax.axis_index("prow"), lax.axis_index("pcol")
    k = k_ref[0]
    n = k + 1
    w1, l21, w2 = split(fac_ref[0]), split(fac_ref[1]), split(fac_ref[2])

    ids = [r, r + 32, c, c + 32, c + 16, c + 48]
    for v, i in enumerate(ids):
        if v < 2:
            a1, a2 = rows_ref[0, v], rows_ref[1, v]
        else:
            a1, a2 = cols_ref[v // 2 - 1, 0, v % 2], cols_ref[v // 2 - 1, 1, v % 2]
        a1 = jnp.where((mask_ref[i, k] == 1) & (i > k), a1, 0.0)
        a2 = jnp.where((mask_ref[i, n] == 1) & (i > n), a2, 0.0)
        p1 = split(dot3(split(a1), w1))
        a2 = jnp.where(i > n, a2 - dot3(p1, l21), 0.0)
        p2 = split(dot3(split(a2), w2))
        l1h[v], l1l[v] = p1
        l2h[v], l2l[v] = p2

    col_slot = [2, 4, 3, 5]
    for s in range(2):
        i = r + 32 * s
        for t in range(4):
            j = c + 16 * t
            v = col_slot[t]
            lower = i >= j
            if s == 0 and t >= 2:
                out_ref[s, :, t, :] = jnp.zeros((B, B), F32)
                continue
            base = jnp.where((mask_ref[i, j] == 1) & lower, m_ref[s, t], 0.0)
            upd = dot3((l1h[s], l1l[s]), (l1h[v], l1l[v])) + dot3((l2h[s], l2l[s]), (l2h[v], l2l[v]))
            out_ref[s, :, t, :] = base - jnp.where(lower, upd, 0.0)

    eye = jnp.where(
        lax.broadcasted_iota(jnp.int32, (B, B), 0) == lax.broadcasted_iota(jnp.int32, (B, B), 1), 1.0, 0.0
    ).astype(F32)
    for s in range(2):
        i = r + 32 * s
        for t in range(3):
            j = c + 16 * t

            @pl.when((j == k) & (i > k))
            def _():
                out_ref[s, :, t, :] = l1h[s].astype(F32) + l1l[s].astype(F32)

            @pl.when((j == n) & (i > n))
            def _():
                out_ref[s, :, t, :] = l2h[s].astype(F32) + l2l[s].astype(F32)

            @pl.when((j == k) & (i == k))
            def _():
                a = m_ref[s, t]
                f = ndot((a + a.T) * 0.5 + eye, fac_ref[0])
                low = lax.broadcasted_iota(jnp.int32, (B, B), 0) >= lax.broadcasted_iota(jnp.int32, (B, B), 1)
                out_ref[s, :, t, :] = jnp.where(low, f, 0.0)

            @pl.when((j == n) & (i == n))
            def _():
                a = m_ref[s, t]
                g = fac_ref[1]
                f = ndot((a + a.T) * 0.5 + eye - ndot(g, g), fac_ref[2])
                low = lax.broadcasted_iota(jnp.int32, (B, B), 0) >= lax.broadcasted_iota(jnp.int32, (B, B), 1)
                out_ref[s, :, t, :] = jnp.where(low, f, 0.0)


def vmem():
    return pl.BlockSpec(memory_space=pltpu.VMEM)


def smem():
    return pl.BlockSpec(memory_space=pltpu.SMEM)


def update_call(first_panel, block_mask, blocks, rows, cols, fac):
    return pl.pallas_call(
        update_kernel,
        out_shape=jax.ShapeDtypeStruct((2, B, 4, B), F32),
        in_specs=[smem(), smem(), vmem(), vmem(), vmem(), vmem()],
        out_specs=vmem(),
        scratch_shapes=[pltpu.VMEM((6, B, B), jnp.bfloat16)] * 4,
        compiler_params=pltpu.CompilerParams(vmem_limit_bytes=48 << 20),
        cost_estimate=pl.CostEstimate(flops=4 * 10**9, bytes_accessed=10**7, transcendentals=0),
        name="update",
    )(first_panel, block_mask, blocks, rows, cols, fac)


def local(matrix, block_mask, first_panel):
    dma = pltpu.SemaphoreType.DMA
    rows, cols, fac, blk = pl.pallas_call(
        gather_kernel,
        out_shape=(
            jax.ShapeDtypeStruct((2, 2, B, B), F32),
            jax.ShapeDtypeStruct((2, 2, 2, B, B), F32),
            jax.ShapeDtypeStruct((3, B, B), F32),
            jax.ShapeDtypeStruct((2, 4, B, B), F32),
        ),
        in_specs=[pl.BlockSpec(memory_space=pl.ANY)] * 2,
        out_specs=(vmem(), vmem(), vmem(), vmem()),
        scratch_shapes=[
            pltpu.SMEM((1,), jnp.int32),
            dma,
            pltpu.VMEM((2, B, B), F32),
            pltpu.VMEM((16, NB, B), F32),
            pltpu.VMEM((16, NB, B), F32),
            pltpu.VMEM((2, 32, NB, B), F32),
            pltpu.VMEM((3, B, B), F32),
            pltpu.VMEM((2, B, B), F32),
            pltpu.VMEM((B, B), F32),
            dma((2, 4)),
            dma((2,)), dma((2,)), dma((2,)), dma((2,)), dma((2,)), dma((2,)), dma, dma, dma, dma, dma((2,)), dma((2,)),
            dma((2, 2)), dma((2, 2)), dma((2, 2)), dma((2, 2)), dma((2, 6)), dma((2, 6)),
        ],
        compiler_params=pltpu.CompilerParams(collective_id=0, has_side_effects=True, vmem_limit_bytes=40 << 20),
        cost_estimate=pl.CostEstimate(flops=10**9, bytes_accessed=10**7, transcendentals=0),
        name="gather_factor",
    )(first_panel, matrix)
    return update_call(first_panel, block_mask, blk, rows, cols, fac)


def solution(mesh):
    spec = P(None, "prow", None, "pcol")
    return jax.shard_map(local, mesh=mesh, in_specs=(spec, P(), P()), out_specs=spec, check_vma=False)
```

```python
import functools
import jax
import jax.numpy as jnp
from jax import lax
from jax.experimental import pallas as pl
from jax.experimental.pallas import tpu as pltpu
from jax.sharding import PartitionSpec as P

MESH = pl.DeviceIdType.MESH
HI = lax.Precision.HIGHEST
F32 = jnp.float32
B = 256
NB = 16


def piece_row(c):
    return NB * ((c % 2) * 8 + ((c // 2) % 2) * 4 + c // 4)


def tdot(a, b):
    return lax.dot_general(a, b, (((0,), (0,)), ((), ())), precision=HI, preferred_element_type=F32)


def ndot(a, b):
    return lax.dot_general(a, b, (((1,), (1,)), ((), ())), precision=HI, preferred_element_type=F32)


def inverse_factor(m, w, hook):
    rows = lax.broadcasted_iota(jnp.int32, (NB, 128), 0)
    lane = lax.broadcasted_iota(jnp.int32, (NB, B), 1)
    sub = lax.broadcasted_iota(jnp.int32, (NB, B), 0)
    nxt = m[0:NB, :]
    for p in range(B // NB):
        p0, q = p * NB, p * NB + NB
        inside = (lane >= p0) & (lane < q)
        t = [jnp.broadcast_to(nxt[:, p0 + c : p0 + c + 1], (NB, 128)) for c in range(NB)]
        x = jnp.where(inside, jnp.where(lane - p0 == sub, 1.0, 0.0), nxt)
        x0, x1 = x[:, :128], x[:, 128:]
        s = jnp.ones((NB, 128), F32)
        for j in range(NB):
            d = jnp.broadcast_to(t[j][j : j + 1, :], (NB, 128))
            s = jnp.where(rows == j, lax.rsqrt(d), s)
            mm = jnp.where(rows > j, t[j], 0.0) * (1.0 / d)
            for c in range(j + 1, NB):
                t[c] = t[c] - mm * jnp.broadcast_to(t[c][j : j + 1, :], (NB, 128))
            x0 = x0 - mm * jnp.broadcast_to(x0[j : j + 1, :], (NB, 128))
            x1 = x1 - mm * jnp.broadcast_to(x1[j : j + 1, :], (NB, 128))
        rr = jnp.concatenate([x0 * s, x1 * s], axis=1)
        w[p0:q, :] = jnp.where(lane < q, rr, 0.0)
        if q < B:
            nxt = jnp.where(inside, 0.0, m[q : q + NB, :]) - tdot(rr[:, q : q + NB], rr)
        if q + NB < B:
            wide = lax.broadcasted_iota(jnp.int32, (B - q - NB, B), 1)
            rest = m[q + NB :, :]
            m[q + NB :, :] = jnp.where((wide >= p0) & (wide < q), 0.0, rest) - tdot(rr[:, q + NB :], rr)
        hook(p)


def gather_kernel(
    k_in, m_ref, rows_ref, cols_ref, fac_ref, blk,
    k_ref, k_sem, xs, rsb0, rsb1, hb, low, g12, work, ld,
    rs_s, rs_r, g_s, g_r, cs_s, cs_r, ag_s, ag_r, sib_s, sib_r, zc_s, zc_r, xc_s, xc_r, xf_s, xf_r,
    w_s, w_r,
):
    rsb = (rsb0, rsb1)
    r, c = lax.axis_index("prow"), lax.axis_index("pcol")
    z, x, y, h = r // 4, r % 4, c // 2, c % 2
    cand = (r % 16) == c
    u, rest = r // 16, r % 16
    to_col = (c + 16 * u, rest)
    below = (r + 31) % 32
    home = (below, below % 16)
    is_sub = ((r + 31) % 16) == c

    def at(dz=0, dx=0, dy=0, core=None):
        zz, xx, yy = (z + dz) % 8, (x + dx) % 4, (y + dy) % 8
        return (zz * 4 + xx, yy * 2 + (h if core is None else core))

    def relay_y(zz, m):
        return (2 * zz + (5, 3)[m] + zz // 4) % 8

    on_line = (y == relay_y(z, 0), y == relay_y(z, 1))
    first_holder = on_line[0] & (x == 0)

    def remote(src, dst, ss, rs, to):
        return pltpu.make_async_remote_copy(
            src_ref=src, dst_ref=dst, send_sem=ss, recv_sem=rs, device_id=to, device_id_type=MESH
        )

    def drain(ref, sem):
        pltpu.make_async_copy(ref, ref, sem).wait()

    k_copy = pltpu.make_async_copy(k_in, k_ref, k_sem)
    k_copy.start()
    loads = [
        pltpu.make_async_copy(m_ref.at[s, :, t, :], blk.at[s, t], ld.at[s, t])
        for t in range(4) for s in range(2)
    ]
    for cp in loads:
        cp.start()
    top = jnp.where(r == 0, 1, 0)
    sub_block = blk.at[top, (below) // 16]
    next_block = blk.at[top, r // 16 + 2 * top]
    bar = pltpu.get_barrier_semaphore()

    def greet(to):
        pl.semaphore_signal(bar, inc=1, device_id=to, device_id_type=MESH)

    for j in range(1, 16):
        greet((r, (c + j) % 16))
    for j in range(1, 8):
        greet(at(dz=j))
    for j in range(1, 4):
        greet(at(dx=j))

    @pl.when(jnp.logical_not(cand))
    def _():
        greet((c + 16 * u, rest))

    @pl.when(cand)
    def _():
        up = (r + 1) % 32
        greet((up, up % 16))
        greet((up, r % 16))

    @pl.when(first_holder | on_line[1])
    def _():
        def one(i, carry):
            greet((i, i % 16))
            return carry

        lax.fori_loop(0, 32, one, 0)

    arrivals = 15 + 7 + 3 + jnp.where(cand, 81, 1) + jnp.where(is_sub, 1, 0)
    mine = pl.ds(pl.multiple_of(piece_row(c), NB), NB)

    def first_sends():
        pl.semaphore_wait(bar, arrivals)

        @pl.when(is_sub)
        def _():
            remote(sub_block, g12.at[0], g_s.at[0], g_r.at[0], home).start()

        @pl.when(cand)
        def _():
            remote(next_block, g12.at[1], g_s.at[1], g_r.at[1], home).start()

        for s in range(2):
            for j in range(1, 16):
                to = (c + j) % 16
                row = pl.multiple_of(piece_row(to), NB)
                remote(xs.at[s, pl.ds(row, NB), :], rsb[s].at[c], rs_s.at[s], rs_r.at[s], (r, to)).start()

    for cp in loads:
        cp.wait()
    k_copy.wait()
    k = k_ref[0]
    slot = jnp.where(c == k % 16, k // 16, (k + 1) // 16)
    xs[...] = blk[:, slot]
    rsb0[c] = xs[0, mine, :]
    rsb1[c] = xs[1, mine, :]
    theirs = pl.ds(pl.multiple_of(piece_row(rest), NB), NB)

    def pick_rows(s):
        drain(rsb[s].at[pl.ds(0, 15)], rs_r.at[s])
        rows_ref[0, s, mine, :] = rsb[s][k % 16]
        rows_ref[1, s, mine, :] = rsb[s][(k + 1) % 16]

        @pl.when(jnp.logical_not(cand))
        def _():
            piece = rows_ref.at[:, s, mine, :]
            remote(piece, cols_ref.at[u, :, s, mine, :], cs_s.at[s], cs_r.at[s], to_col).start()

        @pl.when(cand)
        def _():
            cols_ref[u, :, s, mine, :] = rows_ref[:, s, mine, :]

    def send_y():
        piece = rows_ref.at[:, :, mine, :]
        for j in range(1, 8):
            remote(piece, piece, ag_s, ag_r, at(dy=j)).start()

    def send_z(s):
        piece = cols_ref.at[u, :, s, theirs, :]

        @pl.when(jnp.logical_not(cand))
        def _():
            drain(piece, cs_r.at[s])

        for j in range(1, 8):
            remote(piece, piece, zc_s.at[s], zc_r.at[s], at(dz=j)).start()

    def send_sibling():
        drain(rows_ref.at[:, :, pl.ds(0, 7 * NB), :], ag_r)
        half = rows_ref.at[:, :, pl.ds(pl.multiple_of(128 * h, 128), 128), :]
        remote(half, half, sib_s, sib_r, at(core=1 - h)).start()

    def quarter(xx):
        return pl.ds(pl.multiple_of(NB * (8 * (xx % 2) + 4 * ((xx // 2) % 2)), 64), 64)

    def send_x(s):
        drain(cols_ref.at[0, :, s, pl.ds(0, 7 * NB), :], zc_r.at[s])
        part = cols_ref.at[:, :, s, quarter(x), :]
        remote(part, part, xc_s.at[s, 0], xc_r.at[s, 0], at(dx=1)).start()
        remote(part, part, xc_s.at[s, 1], xc_r.at[s, 1], at(dx=3)).start()

    def forward_x(s):
        for way, dx in ((0, 1), (1, 3)):
            part = cols_ref.at[:, :, s, quarter(x + 4 - dx), :]
            drain(part, xc_r.at[s, way])
            half = cols_ref.at[way, :, s, quarter(x + 4 - dx), :]
            remote(half, half, xf_s.at[s, way], xf_r.at[s, way], at(dx=dx)).start()

    def scatter_factor(f, pieces=range(16)):
        for p in pieces:
            zz, core = p % 8, p // 8
            src = low.at[f, pl.ds(p * NB, NB), :]
            if f < 2:
                to = (zz * 4, relay_y(zz, 0) * 2 + core)
                remote(src, hb.at[f, r], w_s.at[0, f], w_r.at[0, f], to).start()
            else:
                for xx in range(4):
                    to = (zz * 4 + xx, relay_y(zz, 1) * 2 + core)
                    remote(src, hb.at[0, r], w_s.at[1, 0], w_r.at[1, 0], to).start()

    slab = pl.ds(pl.multiple_of(128 * h + NB * z, NB), NB)
    side = pl.ds(pl.multiple_of(128 * h, 128), 128)

    def relay_first(stage):
        piece = fac_ref.at[pl.ds(0, 2), slab, :]
        if stage == 0:

            @pl.when(first_holder)
            def _():
                drain(hb.at[0], w_r.at[0, 0])
                drain(hb.at[1], w_r.at[0, 1])
                fac_ref[0, slab, :] = hb[0, k]
                fac_ref[1, slab, :] = hb[1, k]
                for j in range(1, 4):
                    remote(piece, piece, w_s.at[0, 2], w_r.at[0, 2], at(dx=j)).start()

        elif stage == 1:

            @pl.when(on_line[0])
            def _():
                @pl.when(x != 0)
                def _():
                    drain(piece, w_r.at[0, 2])

                for j in range(1, 8):
                    remote(piece, piece, w_s.at[0, 3], w_r.at[0, 3], at(dy=j)).start()

        elif stage == 2:

            @pl.when(jnp.logical_not(on_line[0]))
            def _():
                drain(piece, w_r.at[0, 3])

            for j in range(1, 8):
                remote(piece, piece, w_s.at[0, 4], w_r.at[0, 4], at(dz=j)).start()
        else:
            drain(fac_ref.at[pl.ds(0, 2), pl.ds(0, 7 * NB), :], w_r.at[0, 4])
            half = fac_ref.at[pl.ds(0, 2), side, :]
            remote(half, half, w_s.at[0, 5], w_r.at[0, 5], at(core=1 - h)).start()

    def relay_last(stage):
        piece = fac_ref.at[2, slab, :]
        if stage == 0:

            @pl.when(on_line[1])
            def _():
                drain(hb.at[0], w_r.at[1, 0])
                fac_ref[2, slab, :] = hb[0, k]
                for j in range(1, 8):
                    remote(piece, piece, w_s.at[1, 3], w_r.at[1, 3], at(dy=j)).start()

        elif stage == 1:

            @pl.when(jnp.logical_not(on_line[1]))
            def _():
                drain(piece, w_r.at[1, 3])

            for j in range(1, 8):
                remote(piece, piece, w_s.at[1, 4], w_r.at[1, 4], at(dz=j)).start()
        else:
            drain(fac_ref.at[2, pl.ds(0, 7 * NB), :], w_r.at[1, 4])
            half = fac_ref.at[2, side, :]
            remote(half, half, w_s.at[1, 5], w_r.at[1, 5], at(core=1 - h)).start()

    eye = jnp.where(
        lax.broadcasted_iota(jnp.int32, (B, B), 0) == lax.broadcasted_iota(jnp.int32, (B, B), 1), 1.0, 0.0
    ).astype(F32)

    @pl.when(cand)
    def _():
        a = blk[0, r // 16]
        work[...] = (a + a.T) * 0.5 + eye

        def first_hook(p):
            if p == 4:
                first_sends()
                scatter_factor(0, range(5))
            elif p > 4:
                scatter_factor(0, [p])
            if p == 15:
                pick_rows(0)

        inverse_factor(work, low.at[0], first_hook)
        drain(g12.at[0], g_r.at[0])
        drain(g12.at[1], g_r.at[1])
        l21 = ndot(g12[0], low[0])
        low[1] = l21
        scatter_factor(1)
        d = g12[1]
        work[...] = (d + d.T) * 0.5 + eye - ndot(l21, l21)


        def second_hook(p):
            scatter_factor(2, [p])
            for when, step in plan:
                if when == p:
                    step()

        plan = (
            (0, lambda: send_z(0)),
            (2, lambda: pick_rows(1)),
            (4, lambda: send_z(1)),
            (5, send_y),
            (11, lambda: send_x(0)),
            (13, lambda: relay_first(1)),
        )
        inverse_factor(work, low.at[2], second_hook)
        send_x(1)
        relay_first(2)

    @pl.when(jnp.logical_not(cand))
    def _():
        first_sends()
        pick_rows(0)
        send_z(0)
        pick_rows(1)
        send_z(1)
        send_y()
        relay_first(0)
        relay_first(1)
        send_x(0)
        send_x(1)
        relay_first(2)
        relay_last(0)

    forward_x(0)
    send_sibling()
    relay_last(1)
    forward_x(1)
    relay_first(3)
    relay_last(2)

    drain(fac_ref.at[pl.ds(0, 2), pl.ds(0, 128), :], w_r.at[0, 5])
    drain(fac_ref.at[2, pl.ds(0, 128), :], w_r.at[1, 5])
    drain(rows_ref.at[:, :, pl.ds(0, 128), :], sib_r)
    for s in range(2):
        for way in range(2):
            drain(cols_ref.at[way, :, s, quarter(x + 2), :], xf_r.at[s, way])

    @pl.when(is_sub)
    def _():
        drain(g12.at[0], g_s.at[0])

    @pl.when(cand)
    def _():
        drain(g12.at[0], g_s.at[1])
        drain(low.at[0], w_s.at[0, 0])
        drain(low.at[0], w_s.at[0, 1])
        drain(hb.at[:, pl.ds(0, 32)], w_s.at[1, 0])

    drain(rows_ref.at[:, :, pl.ds(0, 7 * NB), :], ag_s)
    drain(rows_ref.at[:, :, pl.ds(0, 128), :], sib_s)
    for s in range(2):
        drain(rsb[s].at[pl.ds(0, 15)], rs_s.at[s])

        @pl.when(jnp.logical_not(cand))
        def _():
            drain(rows_ref.at[:, s, mine, :], cs_s.at[s])

        drain(cols_ref.at[0, :, s, pl.ds(0, 7 * NB), :], zc_s.at[s])
        for way in range(2):
            drain(cols_ref.at[:, :, s, quarter(x), :], xc_s.at[s, way])
            drain(cols_ref.at[way, :, s, quarter(x), :], xf_s.at[s, way])

    @pl.when(first_holder)
    def _():
        drain(fac_ref.at[pl.ds(0, 2), pl.ds(0, 3 * NB), :], w_s.at[0, 2])

    @pl.when(on_line[0])
    def _():
        drain(fac_ref.at[pl.ds(0, 2), pl.ds(0, 7 * NB), :], w_s.at[0, 3])

    @pl.when(on_line[1])
    def _():
        drain(fac_ref.at[2, pl.ds(0, 7 * NB), :], w_s.at[1, 3])

    drain(fac_ref.at[pl.ds(0, 2), pl.ds(0, 7 * NB), :], w_s.at[0, 4])
    drain(fac_ref.at[2, pl.ds(0, 7 * NB), :], w_s.at[1, 4])
    drain(fac_ref.at[pl.ds(0, 2), pl.ds(0, 128), :], w_s.at[0, 5])
    drain(fac_ref.at[2, pl.ds(0, 128), :], w_s.at[1, 5])


def split(a):
    hi = a.astype(jnp.bfloat16)
    return hi, (a - hi.astype(F32)).astype(jnp.bfloat16)


def dot3(a, b):
    dims = (((1,), (1,)), ((), ()))
    one = lambda u, v: lax.dot_general(u, v, dims, preferred_element_type=F32)
    return one(a[0], b[0]) + (one(a[0], b[1]) + one(a[1], b[0]))


def update_kernel(k_ref, mask_ref, m_ref, rows_ref, cols_ref, fac_ref, out_ref, l1h, l1l, l2h, l2l):
    r, c = lax.axis_index("prow"), lax.axis_index("pcol")
    k = k_ref[0]
    n = k + 1
    w1, l21, w2 = split(fac_ref[0]), split(fac_ref[1]), split(fac_ref[2])

    ids = [r, r + 32, c, c + 32, c + 16, c + 48]
    for v, i in enumerate(ids):
        if v < 2:
            a1, a2 = rows_ref[0, v], rows_ref[1, v]
        else:
            a1, a2 = cols_ref[v // 2 - 1, 0, v % 2], cols_ref[v // 2 - 1, 1, v % 2]
        a1 = jnp.where((mask_ref[i, k] == 1) & (i > k), a1, 0.0)
        a2 = jnp.where((mask_ref[i, n] == 1) & (i > n), a2, 0.0)
        p1 = split(dot3(split(a1), w1))
        a2 = jnp.where(i > n, a2 - dot3(p1, l21), 0.0)
        p2 = split(dot3(split(a2), w2))
        l1h[v], l1l[v] = p1
        l2h[v], l2l[v] = p2

    col_slot = [2, 4, 3, 5]
    for s in range(2):
        i = r + 32 * s
        for t in range(4):
            j = c + 16 * t
            v = col_slot[t]
            lower = i >= j
            if s == 0 and t >= 2:
                out_ref[s, :, t, :] = jnp.zeros((B, B), F32)
                continue
            base = jnp.where((mask_ref[i, j] == 1) & lower, m_ref[s, t], 0.0)
            upd = dot3((l1h[s], l1l[s]), (l1h[v], l1l[v])) + dot3((l2h[s], l2l[s]), (l2h[v], l2l[v]))
            out_ref[s, :, t, :] = base - jnp.where(lower, upd, 0.0)

    eye = jnp.where(
        lax.broadcasted_iota(jnp.int32, (B, B), 0) == lax.broadcasted_iota(jnp.int32, (B, B), 1), 1.0, 0.0
    ).astype(F32)
    for s in range(2):
        i = r + 32 * s
        for t in range(3):
            j = c + 16 * t

            @pl.when((j == k) & (i > k))
            def _():
                out_ref[s, :, t, :] = l1h[s].astype(F32) + l1l[s].astype(F32)

            @pl.when((j == n) & (i > n))
            def _():
                out_ref[s, :, t, :] = l2h[s].astype(F32) + l2l[s].astype(F32)

            @pl.when((j == k) & (i == k))
            def _():
                a = m_ref[s, t]
                f = ndot((a + a.T) * 0.5 + eye, fac_ref[0])
                low = lax.broadcasted_iota(jnp.int32, (B, B), 0) >= lax.broadcasted_iota(jnp.int32, (B, B), 1)
                out_ref[s, :, t, :] = jnp.where(low, f, 0.0)

            @pl.when((j == n) & (i == n))
            def _():
                a = m_ref[s, t]
                g = fac_ref[1]
                f = ndot((a + a.T) * 0.5 + eye - ndot(g, g), fac_ref[2])
                low = lax.broadcasted_iota(jnp.int32, (B, B), 0) >= lax.broadcasted_iota(jnp.int32, (B, B), 1)
                out_ref[s, :, t, :] = jnp.where(low, f, 0.0)


def vmem():
    return pl.BlockSpec(memory_space=pltpu.VMEM)


def smem():
    return pl.BlockSpec(memory_space=pltpu.SMEM)


def update_call(first_panel, block_mask, blocks, rows, cols, fac):
    return pl.pallas_call(
        update_kernel,
        out_shape=jax.ShapeDtypeStruct((2, B, 4, B), F32),
        in_specs=[smem(), smem(), vmem(), vmem(), vmem(), vmem()],
        out_specs=vmem(),
        scratch_shapes=[pltpu.VMEM((6, B, B), jnp.bfloat16)] * 4,
        compiler_params=pltpu.CompilerParams(vmem_limit_bytes=48 << 20),
        cost_estimate=pl.CostEstimate(flops=4 * 10**9, bytes_accessed=10**7, transcendentals=0),
        name="update",
    )(first_panel, block_mask, blocks, rows, cols, fac)


def local(matrix, block_mask, first_panel):
    dma = pltpu.SemaphoreType.DMA
    rows, cols, fac, blk = pl.pallas_call(
        gather_kernel,
        out_shape=(
            jax.ShapeDtypeStruct((2, 2, B, B), F32),
            jax.ShapeDtypeStruct((2, 2, 2, B, B), F32),
            jax.ShapeDtypeStruct((3, B, B), F32),
            jax.ShapeDtypeStruct((2, 4, B, B), F32),
        ),
        in_specs=[pl.BlockSpec(memory_space=pl.ANY)] * 2,
        out_specs=(vmem(), vmem(), vmem(), vmem()),
        scratch_shapes=[
            pltpu.SMEM((1,), jnp.int32),
            dma,
            pltpu.VMEM((2, B, B), F32),
            pltpu.VMEM((16, NB, B), F32),
            pltpu.VMEM((16, NB, B), F32),
            pltpu.VMEM((2, 32, NB, B), F32),
            pltpu.VMEM((3, B, B), F32),
            pltpu.VMEM((2, B, B), F32),
            pltpu.VMEM((B, B), F32),
            dma((2, 4)),
            dma((2,)), dma((2,)), dma((2,)), dma((2,)), dma((2,)), dma((2,)), dma, dma, dma, dma, dma((2,)), dma((2,)),
            dma((2, 2)), dma((2, 2)), dma((2, 2)), dma((2, 2)), dma((2, 6)), dma((2, 6)),
        ],
        compiler_params=pltpu.CompilerParams(collective_id=0, has_side_effects=True, vmem_limit_bytes=40 << 20),
        cost_estimate=pl.CostEstimate(flops=10**9, bytes_accessed=10**7, transcendentals=0),
        name="gather_factor",
    )(first_panel, matrix)
    return update_call(first_panel, block_mask, blk, rows, cols, fac)


def solution(mesh):
    spec = P(None, "prow", None, "pcol")
    return jax.shard_map(local, mesh=mesh, in_specs=(spec, P(), P()), out_specs=spec, check_vma=False)
```
